32 devices in a mesh: group: 2 (over y), swap: 8 (over z, x), image: 2 (over core).
Axes of the slice: x: 2, y: 2, z: 4, core: 2. Of those that a mesh axis runs over, the one named last changes fastest.
Arguments:
- images_in: bfloat16 [16, 1536, 4096], P(('group', 'image'), 'swap'), parts along dimension 0, may hold values from -6 to 6
- kernel: bfloat16 [1536, 49], P('swap'), may hold values from -1.75 to 1.75
- conv_bias: float32 [1536], P('swap'), may hold values from -1 to 1
- norm_gain: float32 [1536], replicated, may hold values from 0.1 to 1.9
- norm_shift: float32 [1536], replicated, may hold values from -0.5 to 0.5
- fp8_weight: bfloat16 [1536, 6144], P('swap', 'image'), may hold values from -1.875 to 1.875, as said below
- block_scale: int32 [1536, 48], P('swap', 'image'), may hold values from -7 to -5
- adapter_a: bfloat16 [1536, 32], replicated, may hold values from -0.15625 to 0.15625
- adapter_b: bfloat16 [32, 6144], P(None, 'image'), may hold values from -0.25 to 0.25
- cotangent: bfloat16 [16, 4096, 6144], P('group', 'swap', 'image'), parts along dimension 0, may hold values from -0.05 to 0.05
Outputs:
- grad_a: float32 [3072, 32], P('group'), parts along dimension 0
- grad_b: float32 [64, 6144], P('group', 'image'), parts along dimension 0
The draws below stay inside these ranges and needn't reach their ends.
There are 2 independent parts, one for each index of `group`. The reference program is written for one: setup_inputs(seed, part) draws one part's arguments, and reference() takes and returns one part's arrays. A program takes and returns all parts, laid end to end along the dimension named above; an argument that names none is the same for every part. Nothing has to cross between parts.
Inputs may be any that keep to these rules, and one draw needn't show every extreme that they name: `fp8_weight`: each entry is a value of the E4M3 format: a sign times 2 to an integer power times 1 + k / 8 for an integer k of 0 to 7. `block_scale`: the entry at [c, j] is the exponent of the scale of hidden units 128 * j to 128 * j + 127 of weight row c.
All inputs are finite; a program needn't handle non-finite values.
Results may differ from the reference program's by a relative error of at most 0.00055.
The reference program's roundings to bfloat16 on the way (of `conv`, `normed`, `scaled_weight`, `low_rank` and `grad_pre`) count: a program that leaves them out, or rounds other values in their place, can miss the bound.
Values may be sent and summed in bfloat16 or wider, within the bound.
No kernel may reach another device: no remote copies, remote signals or barrier semaphores. Data moves between devices by JAX's collectives and lax.ppermute only.
A program may use at most 192 MiB of HBM per device.

```python
import math
import jax
import jax.numpy as jnp
from jax import lax

C = 1536
FF = 6144
R = 32
KS = 7
H = 64
W = 64
IMAGES = 8


def draw_kernel(key, part):
    first_key, second_key = jax.random.split(key)
    spread = jnp.exp(jax.random.uniform(second_key, (C, 1), jnp.float32, math.log(0.3), math.log(3.0)))
    values = jnp.clip(jax.random.normal(first_key, (C, KS * KS), jnp.float32), -4.0, 4.0)
    return (values * spread / KS).astype(jnp.bfloat16)


def draw_fp8_weight(key, part):
    sign_key, power_key, mantissa_key = jax.random.split(key, 3)
    lowest = -2
    negative = jax.random.bernoulli(sign_key, 0.5, (C, FF))
    exponent = jax.random.randint(power_key, (C, FF), lowest, 1)
    mantissa = jax.random.randint(mantissa_key, (C, FF), 0, 8)
    power = jnp.where(exponent == -3, 0.125, jnp.where(exponent == -2, 0.25, jnp.where(exponent == -1, 0.5, 1.0)))
    signs = jnp.where(negative, -1.0, 1.0)
    values = signs * power * (1.0 + mantissa.astype(jnp.float32) / 8.0)
    return values.astype(jnp.float32).astype(jnp.bfloat16)


def draw_cotangent(key, part):
    value_key, scale_key = jax.random.split(key, 2)
    shape = (IMAGES, H * W, FF)
    row_scale = jnp.exp(jax.random.uniform(scale_key, (IMAGES, H * W, 1), jnp.float32, 0.0, math.log(10.0)))
    values = jnp.clip(jax.random.normal(value_key, shape, jnp.float32), -4.0, 4.0)
    return (values * row_scale / 1024.0).astype(jnp.bfloat16)


def place_ends(entries, stream_key, least, largest):
    place = [jax.random.randint(jax.random.fold_in(stream_key, axis), (), 0, length) for axis, length in enumerate(entries.shape)]
    main_axis = entries.shape.index(max(entries.shape))
    beside = place[:main_axis] + [(place[main_axis] + 1) % entries.shape[main_axis]] + place[main_axis + 1:]
    return entries.at[tuple(place)].set(least).at[tuple(beside)].set(largest)


def steps_of(stream_key, extent, cuts, least, largest):
    level, own = 1.0, jax.random.fold_in(stream_key, 6)
    for position, shards_of in cuts:
        draws = jnp.exp(jax.random.uniform(jax.random.fold_in(own, position), (shards_of,), jnp.float32, least / len(cuts), largest / len(cuts)))
        level = level * jnp.repeat(draws, extent[position] // shards_of).reshape([-1 if axis == position else 1 for axis in range(len(extent))])
    return level


def noise(rng, dims, width, most, pieces=(), dtype=jnp.bfloat16):
    loudness = steps_of(rng, dims, pieces, -0.22, 0.18) if pieces else 1.0
    result = jax.random.normal(rng, dims, jnp.float32) * width * loudness
    return jnp.minimum(jnp.maximum(result, -most), most).astype(dtype)


def setup_inputs(seed: int = 0, part: int = 0) -> dict:
    key_list = jax.random.split(jax.random.key(seed), 11)
    own_keys = jax.random.split(jax.random.fold_in(key_list[10], part), 11)
    images_in = noise(own_keys[0], (IMAGES, C, H * W), 1.0, 6.0, ((0, 2), (1, 8)))
    kernel = draw_kernel(jax.random.fold_in(key_list[10], 71), part)
    conv_bias = jnp.clip(jax.random.uniform(key_list[2], (C,), jnp.float32, -1.0, 1.0) * steps_of(key_list[2], (C,), ((0, 8),), -0.4, 0.0), -1.0, 1.0)
    norm_gain = jnp.clip(1.0 + 0.18 * jax.random.normal(key_list[3], (C,), jnp.float32), 0.1, 1.9)
    norm_shift = jnp.clip(jax.random.uniform(key_list[4], (C,), jnp.float32, -0.5, 0.5), -0.5, 0.5)
    fp8_weight = draw_fp8_weight(jax.random.fold_in(key_list[10], 71), part)
    block_scale = place_ends(jax.random.randint(key_list[6], (C, FF // 128), -7, -4), jax.random.fold_in(key_list[6], 1), -7, (-4) - 1).astype(jnp.int32)
    adapter_a = noise(key_list[7], (C, R), C ** -0.5, 0.15625)
    adapter_b = noise(key_list[8], (R, FF), (R * 16) ** -0.5, 0.25, ((1, 2),))
    cotangent = draw_cotangent(jax.random.fold_in(jax.random.fold_in(key_list[10], part), 71), part)
    return {"images_in": images_in, "kernel": kernel, "conv_bias": conv_bias, "norm_gain": norm_gain, "norm_shift": norm_shift, "fp8_weight": fp8_weight, "block_scale": block_scale, "adapter_a": adapter_a, "adapter_b": adapter_b, "cotangent": cotangent}


adapter_scale = 2.0
norm_eps = 1e-06

def power_table(scales):
    factor = jnp.zeros(scales.shape, jnp.float32)
    for exponent in range(-12, 4):
        factor = factor + jnp.where(scales == exponent, jnp.float32(2.0 ** exponent), jnp.float32(0.0))
    return factor

def decode(weight, scales):
    row_count = weight.shape[0]
    groups = scales.shape[1]
    blocks = weight.reshape(row_count, groups, -1).astype(jnp.float32) * power_table(scales)[:, :, None]
    return blocks.reshape(row_count, -1).astype(jnp.bfloat16)

def gelu_slope(pre_act):
    cumulative = 0.5 * (1.0 + jax.scipy.special.erf(pre_act * 0.7071067811865476))
    density = jnp.exp(-0.5 * pre_act * pre_act) * 0.3989422804014327
    return cumulative + pre_act * density

def depthwise(images, kernel, conv_bias, map_width):
    pixels = images.shape[-1]
    last_axis = images.ndim - 1
    half_span = KS // 2
    margin = half_span * map_width + half_span
    padded = jnp.pad(images, [(0, 0)] * last_axis + [(margin, margin)])
    column = jnp.arange(pixels) % map_width
    weights = kernel.astype(jnp.float32)
    summed = jnp.zeros(images.shape, jnp.float32)
    for row_step in range(KS):
        for col_step in range(KS):
            offset = (row_step - half_span) * map_width + (col_step - half_span)
            shifted = lax.slice_in_dim(padded, margin + offset, margin + offset + pixels, axis=last_axis)
            moved = column + (col_step - half_span)
            inside = ((moved >= 0) & (moved < map_width)).astype(jnp.float32)
            summed = summed + shifted.astype(jnp.float32) * weights[:, row_step * KS + col_step][:, None] * inside
    return summed + conv_bias.astype(jnp.float32)[:, None]

def reference(images_in, kernel, conv_bias, norm_gain, norm_shift, fp8_weight, block_scale, adapter_a, adapter_b, cotangent):
    scaled_weight = decode(fp8_weight, block_scale)

    def one_image(carry, inputs):
        image, upstream = inputs
        conv = depthwise(image, kernel, conv_bias, W).astype(jnp.bfloat16)
        values = conv.astype(jnp.float32)
        average = lax.optimization_barrier(jnp.mean(values, axis=0, keepdims=True))
        centred = values - average
        variance = lax.optimization_barrier(jnp.mean(centred * centred, axis=0, keepdims=True))
        scaled = centred * lax.rsqrt(variance + norm_eps) * norm_gain[:, None] + norm_shift[:, None]
        normed = scaled.T.astype(jnp.bfloat16)
        low_rank = jnp.dot(normed, adapter_a, preferred_element_type=jnp.float32).astype(jnp.bfloat16)
        pre_act = jnp.dot(normed, scaled_weight, preferred_element_type=jnp.float32)
        pre_act = pre_act + adapter_scale * jnp.dot(low_rank, adapter_b, preferred_element_type=jnp.float32)
        grad_pre = (upstream.astype(jnp.float32) * gelu_slope(pre_act)).astype(jnp.bfloat16)
        grad_b = adapter_scale * jnp.dot(low_rank.T, grad_pre, preferred_element_type=jnp.float32)
        back_low = jnp.dot(grad_pre, adapter_b.T, preferred_element_type=jnp.float32)
        grad_a = adapter_scale * jnp.dot(normed.astype(jnp.float32).T, back_low, precision=lax.Precision.HIGHEST)
        return ((carry[0] + grad_a, carry[1] + grad_b), None)
    initial = (jnp.zeros((C, R), jnp.float32), jnp.zeros((R, FF), jnp.float32))
    totals, unused = lax.scan(one_image, initial, (images_in, cotangent))
    return (totals[0], totals[1])
```

```python
import functools

import jax
import jax.numpy as jnp
from jax import lax
from jax.experimental import pallas as pl
from jax.experimental.pallas import tpu as pltpu
from jax.sharding import PartitionSpec as P

KS = 7
W = 64
LANES = 128
HALF = KS // 2

adapter_scale = 2.0
norm_eps = 1e-06

TAIL_STEP = 0.275
TAIL = (0.11780931, 0.04211112, 0.33393318, -0.33099448, 0.45199936, -0.11485849)
DENSITY = 0.3989422804014327
VMEM_LIMIT = 56 * 1024 * 1024


def power_table(scales):
    factor = jnp.zeros(scales.shape, jnp.float32)
    for exponent in range(-12, 4):
        factor = factor + jnp.where(
            scales == exponent, jnp.float32(2.0**exponent), jnp.float32(0.0)
        )
    return factor


def decode(weight, scales):
    row_count = weight.shape[0]
    groups = scales.shape[1]
    blocks = (
        weight.reshape(row_count, groups, -1).astype(jnp.float32) * power_table(scales)[:, :, None]
    )
    return blocks.reshape(row_count, -1).astype(jnp.bfloat16)


def params(**more):
    return pltpu.CompilerParams(vmem_limit_bytes=VMEM_LIMIT, **more)


def conv_body(where, image, taps, bias, *rest, parts, tile_rows):
    outs, (padded, coefs, sums) = rest[:parts], rest[parts:]
    channels, pixels = image.shape[1:]
    tiles = pixels // LANES
    span = pixels // parts
    margin = 2 * LANES
    padded[:, :margin] = jnp.zeros((channels, margin), jnp.float32)
    padded[:, margin + pixels :] = jnp.zeros((channels, margin), jnp.float32)
    padded[:, margin : margin + pixels] = image[0].astype(jnp.float32)
    wide = taps[...].astype(jnp.float32)
    for tap in range(KS * KS):
        coefs[tap] = jnp.broadcast_to(wide[:, tap : tap + 1], (channels, LANES))
    lane = lax.broadcasted_iota(jnp.int32, (8, LANES), 1)
    column = lane % W
    first = lane < W

    def some(step, carry):
        group, block = step // (tiles // tile_rows), step % (tiles // tile_rows)
        rows = pl.ds(pl.multiple_of(group * 8, 8), 8)
        start = block * (tile_rows * LANES)
        count = tile_rows + 4
        raw = [
            padded[rows, pl.ds(pl.multiple_of(start + i * LANES, LANES), LANES)]
            for i in range(count)
        ]
        base = jnp.broadcast_to(bias[rows, :], (8, LANES))
        total = [base] * tile_rows
        for b in range(KS):
            shift = b - HALF
            if shift:
                moved = column + shift
                inside = (moved >= 0) & (moved < W)
                lined = [
                    jnp.where(inside, pltpu.roll(tile, (-shift) % LANES, 1), 0.0) for tile in raw
                ]
            else:
                lined = raw
            for row_step in (-2, 0, 2):
                coef = coefs[(row_step + HALF) * KS + b, rows, :]
                for j in range(tile_rows):
                    total[j] = total[j] + lined[j + 2 + row_step // 2] * coef
            turned = [pltpu.roll(tile, W, 1) for tile in lined]
            between = [jnp.where(first, turned[i], turned[i + 1]) for i in range(count - 1)]
            for row_step in (-3, -1, 1, 3):
                coef = coefs[(row_step + HALF) * KS + b, rows, :]
                for j in range(tile_rows):
                    total[j] = total[j] + between[j + 2 + (row_step - 1) // 2] * coef
        for j in range(tile_rows):
            sums[rows, pl.ds(pl.multiple_of(start + j * LANES, LANES), LANES)] = total[j]
        return carry

    lax.fori_loop(0, (channels // 8) * (tiles // tile_rows), some, 0)
    for k in range(parts):
        origin = pl.multiple_of(lax.bitwise_xor(where[0], k) * span, LANES)
        outs[k][...] = sums[:, pl.ds(origin, span)].astype(jnp.bfloat16)


def conv_image(index, place, images, kernel, conv_bias, parts):
    _, channels, pixels = images.shape
    rows = 16
    tiles = pixels // LANES
    tile_rows = 16 if tiles % 16 == 0 else 1
    span = pixels // parts
    return pl.pallas_call(
        functools.partial(conv_body, parts=parts, tile_rows=tile_rows),
        grid_spec=pltpu.PrefetchScalarGridSpec(
            num_scalar_prefetch=1,
            grid=(channels // rows,),
            in_specs=[
                pl.BlockSpec((1, rows, pixels), lambda c, place: (index, c, 0)),
                pl.BlockSpec((rows, KS * KS), lambda c, place: (c, 0)),
                pl.BlockSpec((rows, 1), lambda c, place: (c, 0)),
            ],
            out_specs=[pl.BlockSpec((rows, span), lambda c, place: (c, 0))] * parts,
            scratch_shapes=[
                pltpu.VMEM((rows, pixels + 4 * LANES), jnp.float32),
                pltpu.VMEM((KS * KS, rows, LANES), jnp.float32),
                pltpu.VMEM((rows, pixels), jnp.float32),
            ],
        ),
        out_shape=[jax.ShapeDtypeStruct((channels, span), jnp.bfloat16)] * parts,
        compiler_params=params(),
        name=f"conv_{index}",
    )(place, images, kernel, conv_bias)


def norm_body(where, *refs, parts):
    pieces, (gain, shift, out, values) = refs[:parts], refs[parts:]
    rows = pieces[0].shape[0]
    for k in range(parts):
        origin = pl.multiple_of(lax.bitwise_xor(where[0], k) * rows, 16)
        values[pl.ds(origin, rows), :] = pieces[k][...].astype(jnp.float32)
    channels = values.shape[0]
    average = jnp.sum(values[...], axis=0, keepdims=True) * (1.0 / channels)
    centred = values[...] - average
    variance = jnp.sum(centred * centred, axis=0, keepdims=True) * (1.0 / channels)
    scaled = centred * lax.rsqrt(variance + norm_eps) * gain[...] + shift[...]
    out[...] = scaled.astype(jnp.bfloat16).T


def norm_image(index, place, pieces, gain, shift):
    parts = len(pieces)
    rows, span = pieces[0].shape
    channels = rows * parts
    width = LANES
    return pl.pallas_call(
        functools.partial(norm_body, parts=parts),
        grid_spec=pltpu.PrefetchScalarGridSpec(
            num_scalar_prefetch=1,
            grid=(span // width,),
            in_specs=[pl.BlockSpec((rows, width), lambda p, place: (0, p))] * parts
            + [pl.BlockSpec((channels, 1), lambda p, place: (0, 0))] * 2,
            out_specs=pl.BlockSpec((width, channels), lambda p, place: (p, 0)),
            scratch_shapes=[pltpu.VMEM((channels, width), jnp.float32)],
        ),
        out_shape=jax.ShapeDtypeStruct((span, channels), jnp.bfloat16),
        compiler_params=params(),
        name=f"norm_{index}",
    )(place, *pieces, gain, shift)


def gelu_slope(x):
    size = jnp.abs(x)
    t = 1.0 / (1.0 + TAIL_STEP * size)
    tail = TAIL[-1]
    for coefficient in TAIL[-2::-1]:
        tail = tail * t + coefficient
    fall = jnp.exp(-0.5 * (x * x)) * (DENSITY * size - tail * t)
    return jnp.where(x >= 0, 1.0 + fall, -fall)


def main_body(where, own, other, weight, down, up, cot_own, cot_other, grad_a, grad_b, low, low_t, back, pre, *, step):
    f = pl.program_id(0)
    span = own.shape[0]
    sides = ((own, cot_own, 0), (other, cot_other, span))

    @pl.when(f == 0)
    def first():
        for tokens, _, base in sides:
            product = jnp.dot(tokens[...], down[...], preferred_element_type=jnp.float32)
            rounded = product.astype(jnp.bfloat16).astype(jnp.float32) * adapter_scale
            low[base : base + span, :] = rounded.astype(jnp.bfloat16)
            low_t[:, base : base + span] = rounded.T.astype(jnp.bfloat16)
        back[...] = jnp.zeros_like(back)

    blocks = [
        (tokens, cot, start, base + start)
        for tokens, cot, base in sides
        for start in range(0, span, step)
    ]
    grad_b_total = None

    def project(n):
        tokens, _, start, place = blocks[n]
        pre[n % 2] = jnp.dot(
            tokens[start : start + step, :], weight[...], preferred_element_type=jnp.float32
        ) + jnp.dot(low[place : place + step, :], up[...], preferred_element_type=jnp.float32)

    project(0)
    for n, (_, cot, start, place) in enumerate(blocks):
        if n + 1 < len(blocks):
            project(n + 1)
        slope = gelu_slope(pre[n % 2])
        grad_pre = (cot[0, start : start + step, :].astype(jnp.float32) * slope).astype(jnp.bfloat16)
        product = jnp.dot(
            low_t[:, place : place + step], grad_pre, preferred_element_type=jnp.float32
        )
        grad_b_total = product if grad_b_total is None else grad_b_total + product
        back[:, place : place + step] += lax.dot_general(
            up[...], grad_pre, (((1,), (1,)), ((), ())), preferred_element_type=jnp.float32
        )
    grad_b[...] = grad_b_total

    @pl.when(f == pl.num_programs(0) - 1)
    def last():
        rank = back.shape[0]
        total = None
        for tokens, _, base in sides:
            wide = back[:, base : base + span] * adapter_scale
            high = wide.astype(jnp.bfloat16)
            rest = (wide - high.astype(jnp.float32)).astype(jnp.bfloat16)
            both = jnp.concatenate([high, rest], axis=0)
            product = jnp.dot(both, tokens[...], preferred_element_type=jnp.float32)
            total = product if total is None else total + product
        grad_a[...] = total[:rank] + total[rank:]


def main_chunk(index, place, own, other, weight, down, up, cotangent):
    span, channels = own.shape
    hidden = weight.shape[1]
    rank = down.shape[1]
    half = cotangent.shape[0] // 2
    width = 512 if hidden % 512 == 0 else LANES
    step = 256 if span % 256 == 0 else span
    return pl.pallas_call(
        functools.partial(main_body, step=step),
        grid_spec=pltpu.PrefetchScalarGridSpec(
            num_scalar_prefetch=1,
            grid=(hidden // width,),
            in_specs=[
                pl.BlockSpec((span, channels), lambda f, place: (0, 0)),
                pl.BlockSpec((span, channels), lambda f, place: (0, 0)),
                pl.BlockSpec((channels, width), lambda f, place: (0, f)),
                pl.BlockSpec((channels, rank), lambda f, place: (0, 0)),
                pl.BlockSpec((rank, width), lambda f, place: (0, f)),
                pl.BlockSpec((1, span, width), lambda f, place: (place[1] * half + index, 0, f)),
                pl.BlockSpec((1, span, width), lambda f, place: ((1 - place[1]) * half + index, 0, f)),
            ],
            out_specs=[
                pl.BlockSpec((rank, channels), lambda f, place: (0, 0)),
                pl.BlockSpec((rank, width), lambda f, place: (0, f)),
            ],
            scratch_shapes=[
                pltpu.VMEM((2 * span, rank), jnp.bfloat16),
                pltpu.VMEM((rank, 2 * span), jnp.bfloat16),
                pltpu.VMEM((rank, 2 * span), jnp.float32),
                pltpu.VMEM((2, step, width), jnp.float32),
            ],
        ),
        out_shape=[
            jax.ShapeDtypeStruct((rank, channels), jnp.float32),
            jax.ShapeDtypeStruct((rank, hidden), jnp.float32),
        ],
        compiler_params=params(),
        name=f"main_{index}",
    )(place, own, other, weight, down, up, cotangent, cotangent)


def across(parts, k):
    return [(s, s ^ k) for s in range(parts)]


def total_over_swap(parts, me, share):
    mine = lax.dynamic_index_in_dim(share, me, 0, keepdims=False)
    got = [
        lax.ppermute(
            lax.dynamic_index_in_dim(share, lax.bitwise_xor(me, k), 0, keepdims=False),
            "swap",
            across(parts, k),
        )
        for k in range(parts - 1, 0, -1)
    ]
    for piece in got:
        mine = mine + piece
    whole = jnp.zeros(share.shape, share.dtype)
    whole = lax.dynamic_update_index_in_dim(whole, mine, me, 0)
    for k in range(parts - 1, 0, -1):
        piece = lax.ppermute(mine, "swap", across(parts, k))
        whole = lax.dynamic_update_index_in_dim(whole, piece, lax.bitwise_xor(me, k), 0)
    return whole


def shards_kernels(
    parts,
    images_in,
    kernel,
    conv_bias,
    norm_gain,
    norm_shift,
    fp8_weight,
    block_scale,
    adapter_a,
    adapter_b,
    cotangent,
):
    me = lax.axis_index("swap")
    side = lax.axis_index("image")
    place = jnp.stack([me, side]).astype(jnp.int32)
    local_weight = decode(fp8_weight, block_scale)
    weight = lax.all_gather(local_weight, "swap", axis=0, tiled=True)
    bias, gain, shift = conv_bias[:, None], norm_gain[:, None], norm_shift[:, None]
    grad_a, grad_b = [], []
    for index in range(images_in.shape[0]):
        pieces = conv_image(index, place, images_in, kernel, bias, parts)
        arrived = [pieces[0]] + [
            lax.ppermute(pieces[k], "swap", across(parts, k)) for k in range(1, parts)
        ]
        own = norm_image(index, place, arrived, gain, shift)
        other = lax.ppermute(own, "image", [(0, 1), (1, 0)])
        one_a, one_b = main_chunk(
            index, place, own, other, weight, adapter_a, adapter_b, cotangent
        )
        grad_a.append(one_a)
        grad_b.append(one_b)
    rank = adapter_a.shape[1]
    sum_a, sum_b = sum(grad_a[1:], grad_a[0]), sum(grad_b[1:], grad_b[0])
    half = sum_a.shape[1] // 2
    halves = sum_a.reshape(rank, 2, half).swapaxes(0, 1)
    kept = lax.dynamic_index_in_dim(halves, side, 0, keepdims=False)
    given = lax.dynamic_index_in_dim(halves, 1 - side, 0, keepdims=False)
    kept = kept + lax.ppermute(given, "image", [(0, 1), (1, 0)])
    joined = jnp.concatenate([kept, sum_b], axis=1)
    share = joined.reshape(rank, parts, -1).swapaxes(0, 1)
    whole = total_over_swap(parts, me, share).swapaxes(0, 1).reshape(rank, -1)
    kept, sum_b = whole[:, :half], whole[:, half:]
    given = lax.ppermute(kept, "image", [(0, 1), (1, 0)])
    low = jnp.where(side == 0, kept, given)
    high = jnp.where(side == 0, given, kept)
    return jnp.concatenate([low, high], axis=1).T, sum_b


def shards_plain(
    images_in,
    kernel,
    conv_bias,
    norm_gain,
    norm_shift,
    fp8_weight,
    block_scale,
    adapter_a,
    adapter_b,
    cotangent,
):
    batch, channels, pixels = images_in.shape
    maps = images_in.reshape(batch, channels, pixels // W, W)
    conv = lax.conv_general_dilated(
        maps,
        kernel.reshape(channels, 1, KS, KS),
        (1, 1),
        ((HALF, HALF), (HALF, HALF)),
        dimension_numbers=("NCHW", "OIHW", "NCHW"),
        feature_group_count=channels,
        preferred_element_type=jnp.float32,
    ).reshape(batch, channels, pixels)
    conv = (conv + conv_bias[None, :, None]).astype(jnp.bfloat16)
    values = lax.all_to_all(conv, "swap", split_axis=2, concat_axis=1, tiled=True).astype(
        jnp.float32
    )
    average = jnp.mean(values, axis=1, keepdims=True)
    centred = values - average
    variance = jnp.mean(centred * centred, axis=1, keepdims=True)
    scaled = (
        centred * lax.rsqrt(variance + norm_eps) * norm_gain[None, :, None]
        + norm_shift[None, :, None]
    )
    normed = jnp.swapaxes(scaled, 1, 2).astype(jnp.bfloat16)
    own_rows = normed.reshape(-1, normed.shape[2])
    tokens = lax.all_gather(own_rows, "image", axis=0, tiled=True)
    local_weight = decode(fp8_weight, block_scale)
    weight = lax.all_gather(local_weight, "swap", axis=0, tiled=True)
    frozen = jnp.dot(tokens, weight, preferred_element_type=jnp.float32)
    low_rank = jnp.dot(tokens, adapter_a, preferred_element_type=jnp.float32).astype(jnp.bfloat16)
    pre_act = frozen + adapter_scale * jnp.dot(
        low_rank, adapter_b, preferred_element_type=jnp.float32
    )
    upstream = cotangent.reshape(-1, cotangent.shape[2])
    cumulative = 0.5 * (1.0 + jax.scipy.special.erf(pre_act * 0.7071067811865476))
    slope = cumulative + pre_act * (jnp.exp(-0.5 * pre_act * pre_act) * DENSITY)
    grad_pre = (upstream.astype(jnp.float32) * slope).astype(jnp.bfloat16)
    grad_b = adapter_scale * jnp.dot(low_rank.T, grad_pre, preferred_element_type=jnp.float32)
    back = lax.psum(jnp.dot(grad_pre, adapter_b.T, preferred_element_type=jnp.float32), "image")
    grad_a = adapter_scale * lax.dot_general(
        tokens.astype(jnp.float32),
        back,
        (((0,), (0,)), ((), ())),
        precision=lax.Precision.HIGHEST,
        preferred_element_type=jnp.float32,
    )
    return lax.psum((grad_a, grad_b), "swap")


def solution(mesh):
    placed = (
        P(("group", "image"), "swap", None),
        P("swap", None),
        P("swap"),
        P(),
        P(),
        P("swap", "image"),
        P("swap", "image"),
        P(),
        P(None, "image"),
        P("group", "swap", "image"),
    )
    parts = mesh.shape["swap"]

    def body(*shards):
        _, channels, pixels = shards[0].shape
        span = pixels // parts
        fits = (
            parts <= 8
            and parts & (parts - 1) == 0
            and mesh.shape["image"] == 2
            and channels % 16 == 0
            and span % LANES == 0
            and LANES % W == 0
            and shards[5].shape[1] % LANES == 0
        )
        return functools.partial(shards_kernels, parts)(*shards) if fits else shards_plain(*shards)

    return jax.shard_map(
        body,
        mesh=mesh,
        in_specs=placed,
        out_specs=(P("group", None), P("group", "image")),
        check_vma=False,
    )
```

```python
import functools

import jax
import jax.numpy as jnp
from jax import lax
from jax.experimental import pallas as pl
from jax.experimental.pallas import tpu as pltpu
from jax.sharding import PartitionSpec as P

KS = 7
W = 64
LANES = 128
HALF = KS // 2

adapter_scale = 2.0
norm_eps = 1e-06

TAIL_STEP = 0.275
TAIL = (0.11780931, 0.04211112, 0.33393318, -0.33099448, 0.45199936, -0.11485849)
DENSITY = 0.3989422804014327
VMEM_LIMIT = 56 * 1024 * 1024


def power_table(scales):
    factor = jnp.zeros(scales.shape, jnp.float32)
    for exponent in range(-12, 4):
        factor = factor + jnp.where(
            scales == exponent, jnp.float32(2.0**exponent), jnp.float32(0.0)
        )
    return factor


def decode(weight, scales):
    row_count = weight.shape[0]
    groups = scales.shape[1]
    blocks = (
        weight.reshape(row_count, groups, -1).astype(jnp.float32) * power_table(scales)[:, :, None]
    )
    return blocks.reshape(row_count, -1).astype(jnp.bfloat16)


def params(**more):
    return pltpu.CompilerParams(vmem_limit_bytes=VMEM_LIMIT, **more)


def shift_table():
    shape = (2 * LANES, 2 * KS, LANES)
    source, case, lane = (lax.broadcasted_iota(jnp.int32, shape, axis) for axis in range(3))
    shift = case // 2 - HALF
    column = lane % W + shift
    hit = (source == lane + shift + W * (case % 2)) & (column >= 0) & (column < W)
    return hit.astype(jnp.bfloat16).reshape(shape[0], -1)


def conv_body(where, image, coefs, bias, table, *rest, parts, group):
    outs, (pairs, lines, sums) = rest[: parts // 2 + 1], rest[parts // 2 + 1 :]
    channels, pixels = image.shape[1:]
    tiles = pixels // LANES
    span = pixels // parts
    zero = jnp.zeros((channels, LANES), jnp.bfloat16)

    def tile(t):
        return image[0, :, t * LANES : (t + 1) * LANES] if 0 <= t < tiles else zero

    for t in range(-2, tiles + 1):
        pairs[t + 2, :, :LANES] = tile(t)
        pairs[t + 2, :, LANES:] = tile(t + 1)

    def prepare(start, stop):
        flat = pairs[start:stop].reshape((stop - start) * channels, 2 * LANES)
        moved = jnp.dot(flat, table[...], preferred_element_type=jnp.float32)
        lines[start:stop] = moved.reshape(stop - start, channels, 2 * KS * LANES)

    def add(start, rows):
        total = [bias[rows, :]] * group
        for b in range(KS):
            for odd, steps in ((0, (-2, 0, 2)), (1, (-3, -1, 1, 3))):
                at = slice((2 * b + odd) * LANES, (2 * b + odd + 1) * LANES)
                near = [lines[start + j, rows, at] for j in range(group + 3)]
                for row_step in steps:
                    coef = coefs[(row_step + HALF) * KS + b, rows, :]
                    ahead = 2 + (row_step - odd) // 2
                    for j in range(group):
                        total[j] = total[j] + near[j + ahead] * coef
        for j in range(group):
            sums[rows, (start + j) * LANES : (start + j + 1) * LANES] = total[j]

    done = 0
    for start in range(0, tiles, group):
        for ahead in (0, group):
            stop = min(tiles + 3, start + ahead + group + 3)
            if stop > done:
                prepare(done, stop)
                done = stop
        for row in range(0, channels, 8):
            add(start, slice(row, row + 8))
    for k in range(parts):
        origin = pl.multiple_of(lax.bitwise_xor(where[0], k) * span, LANES)
        block = sums[:, pl.ds(origin, span)].astype(jnp.bfloat16)
        if k % 2:
            outs[-1][k // 2, 0] = block
        else:
            outs[k // 2][0] = block


def conv_images(start, count, place, images, coefs, bias, table, parts):
    _, channels, pixels = images.shape
    rows = 16
    tiles = pixels // LANES
    span = pixels // parts
    return pl.pallas_call(
        functools.partial(conv_body, parts=parts, group=16 if tiles % 16 == 0 else 1),
        grid_spec=pltpu.PrefetchScalarGridSpec(
            num_scalar_prefetch=1,
            grid=(count, channels // rows),
            in_specs=[
                pl.BlockSpec((1, rows, pixels), lambda i, c, place: (start + i, c, 0)),
                pl.BlockSpec((KS * KS, rows, LANES), lambda i, c, place: (0, c, 0)),
                pl.BlockSpec((rows, LANES), lambda i, c, place: (c, 0)),
                pl.BlockSpec((2 * LANES, 2 * KS * LANES), lambda i, c, place: (0, 0)),
            ],
            out_specs=[pl.BlockSpec((1, rows, span), lambda i, c, place: (i, c, 0))] * (parts // 2)
            + [pl.BlockSpec((parts // 2, 1, rows, span), lambda i, c, place: (0, i, c, 0))],
            scratch_shapes=[
                pltpu.VMEM((tiles + 3, rows, 2 * LANES), jnp.bfloat16),
                pltpu.VMEM((tiles + 3, rows, 2 * KS * LANES), jnp.float32),
                pltpu.VMEM((rows, pixels), jnp.float32),
            ],
        ),
        out_shape=[jax.ShapeDtypeStruct((count, channels, span), jnp.bfloat16)] * (parts // 2)
        + [jax.ShapeDtypeStruct((parts // 2, count, channels, span), jnp.bfloat16)],
        compiler_params=params(),
        name=f"conv_{start}",
    )(place, images, coefs, bias, table)


def norm_body(where, *refs, parts):
    pieces, (gain, shift, out, values) = refs[: parts // 2], refs[parts // 2 :]
    rows = pieces[0].shape[2]
    for k in range(parts):
        origin = pl.multiple_of(lax.bitwise_xor(where[0], k) * rows, 16)
        values[pl.ds(origin, rows), :] = pieces[k // 2][k % 2, 0].astype(jnp.float32)
    channels = values.shape[0]
    average = jnp.sum(values[...], axis=0, keepdims=True) * (1.0 / channels)
    centred = values[...] - average
    variance = jnp.sum(centred * centred, axis=0, keepdims=True) * (1.0 / channels)
    scaled = centred * lax.rsqrt(variance + norm_eps) * gain[...] + shift[...]
    out[...] = scaled.astype(jnp.bfloat16).T


def norm_images(start, place, pieces, gain, shift):
    parts = 2 * len(pieces)
    _, count, rows, span = pieces[0].shape
    channels = rows * parts
    return pl.pallas_call(
        functools.partial(norm_body, parts=parts),
        grid_spec=pltpu.PrefetchScalarGridSpec(
            num_scalar_prefetch=1,
            grid=(count,),
            in_specs=[pl.BlockSpec((2, 1, rows, span), lambda i, place: (0, i, 0, 0))] * (parts // 2)
            + [pl.BlockSpec((channels, 1), lambda i, place: (0, 0))] * 2,
            out_specs=pl.BlockSpec((span, channels), lambda i, place: (i, 0)),
            scratch_shapes=[pltpu.VMEM((channels, span), jnp.float32)],
        ),
        out_shape=jax.ShapeDtypeStruct((count * span, channels), jnp.bfloat16),
        compiler_params=params(),
        name=f"norm_{start}",
    )(place, *pieces, gain, shift)


def gelu_slope(x):
    size = jnp.abs(x)
    t = 1.0 / (1.0 + TAIL_STEP * size)
    tail = TAIL[-1]
    for coefficient in TAIL[-2::-1]:
        tail = tail * t + coefficient
    fall = jnp.exp(-0.5 * (x * x)) * (DENSITY * size - tail * t)
    return jnp.where(x >= 0, 1.0 + fall, -fall)


def main_body(where, *refs, step, last_odd, pieces):
    f = pl.program_id(0)
    steps = pl.num_programs(0) - 1
    owns, others, refs = refs[:pieces], refs[pieces : 2 * pieces], refs[2 * pieces :]
    weight, down, up, up_old, cot_own, cot_other, grad_a, grad_b = refs[:8]
    low, low_t, back, pre_even, pre_odd = refs[8:]
    span = cot_own.shape[1]
    rows = cot_own.shape[0] * span
    sides, blocks = [], []
    for side, (group, cot) in enumerate(((owns, cot_own), (others, cot_other))):
        base = 0
        for tokens in group:
            sides.append((tokens, side * rows + base))
            blocks += [
                (tokens, start, cot, base + start, side * rows + base + start)
                for start in range(0, tokens.shape[0], step)
            ]
            base += tokens.shape[0]

    def project(new, block):
        tokens, start, _, _, place = block
        new[place : place + step, :] = jnp.dot(
            tokens[start : start + step, :], weight[...], preferred_element_type=jnp.float32
        ) + jnp.dot(low[place : place + step, :], up[...], preferred_element_type=jnp.float32)

    def finish(old, block):
        _, _, cot, at, place = block
        within = at % span
        upstream = cot[at // span, within : within + step, :].astype(jnp.float32)
        slope = gelu_slope(old[place : place + step, :])
        grad_pre = (upstream * slope).astype(jnp.bfloat16)
        back[:, place : place + step] += lax.dot_general(
            up_old[...], grad_pre, (((1,), (1,)), ((), ())), preferred_element_type=jnp.float32
        )
        return jnp.dot(low_t[:, place : place + step], grad_pre, preferred_element_type=jnp.float32)

    @pl.when(f == 0)
    def first():
        back[...] = jnp.zeros_like(back)
        for tokens, start, _, _, place in blocks:
            product = jnp.dot(
                tokens[start : start + step, :], down[...], preferred_element_type=jnp.float32
            )
            rounded = product.astype(jnp.bfloat16).astype(jnp.float32) * adapter_scale
            low[place : place + step, :] = rounded.astype(jnp.bfloat16)
            low_t[:, place : place + step] = rounded.T.astype(jnp.bfloat16)
        for block in blocks:
            project(pre_even, block)

    def both(new, old):
        total = None
        for block in blocks:
            project(new, block)
            product = finish(old, block)
            total = product if total is None else total + product
        grad_b[...] = total

    inner = (f > 0) & (f < steps)
    pl.when(inner & (f % 2 == 1))(lambda: both(pre_odd, pre_even))
    pl.when(inner & (f % 2 == 0))(lambda: both(pre_even, pre_odd))

    @pl.when(f == steps)
    def last():
        total = None
        for block in blocks:
            product = finish(pre_odd if last_odd else pre_even, block)
            total = product if total is None else total + product
        grad_b[...] = total
        rank = back.shape[0]
        total = None
        for tokens, base in sides:
            wide = back[:, base : base + tokens.shape[0]] * adapter_scale
            high = wide.astype(jnp.bfloat16)
            rest = (wide - high.astype(jnp.float32)).astype(jnp.bfloat16)
            pair = jnp.concatenate([high, rest], axis=0)
            product = jnp.dot(pair, tokens[...], preferred_element_type=jnp.float32)
            total = product if total is None else total + product
        grad_a[...] = total[:rank] + total[rank:]


def main_chunk(index, place, own, other, weight, down, up, cotangent):
    rows, channels = sum(piece.shape[0] for piece in own), own[0].shape[1]
    hidden = weight.shape[1]
    rank = down.shape[1]
    images, span, _ = cotangent.shape
    count = rows // span
    half = images // 2 // count
    at = index // count
    width = 512 if hidden % 512 == 0 else LANES
    step = 256 if span % 256 == 0 else span
    steps = hidden // width

    def now(f):
        return jnp.minimum(f, steps - 1)

    def before(f):
        return jnp.maximum(f - 1, 0)

    return pl.pallas_call(
        functools.partial(main_body, step=step, last_odd=steps % 2 == 0, pieces=len(own)),
        grid_spec=pltpu.PrefetchScalarGridSpec(
            num_scalar_prefetch=1,
            grid=(steps + 1,),
            in_specs=[
                *[pl.BlockSpec(piece.shape, lambda f, place: (0, 0)) for piece in own + other],
                pl.BlockSpec((channels, width), lambda f, place: (0, now(f))),
                pl.BlockSpec((channels, rank), lambda f, place: (0, 0)),
                pl.BlockSpec((rank, width), lambda f, place: (0, now(f))),
                pl.BlockSpec((rank, width), lambda f, place: (0, before(f))),
                pl.BlockSpec((count, span, width), lambda f, place: (place[1] * half + at, 0, before(f))),
                pl.BlockSpec(
                    (count, span, width), lambda f, place: ((1 - place[1]) * half + at, 0, before(f))
                ),
            ],
            out_specs=[
                pl.BlockSpec((rank, channels), lambda f, place: (0, 0)),
                pl.BlockSpec((rank, width), lambda f, place: (0, before(f))),
            ],
            scratch_shapes=[
                pltpu.VMEM((2 * rows, rank), jnp.bfloat16),
                pltpu.VMEM((rank, 2 * rows), jnp.bfloat16),
                pltpu.VMEM((rank, 2 * rows), jnp.float32),
                pltpu.VMEM((2 * rows, width), jnp.float32),
                pltpu.VMEM((2 * rows, width), jnp.float32),
            ],
        ),
        out_shape=[
            jax.ShapeDtypeStruct((rank, channels), jnp.float32),
            jax.ShapeDtypeStruct((rank, hidden), jnp.float32),
        ],
        compiler_params=params(),
        name=f"main_{index}",
    )(place, *own, *other, weight, down, up, up, cotangent, cotangent)


def across(parts, k):
    return [(s, s ^ k) for s in range(parts)]


def after(place, value):
    return lax.optimization_barrier((place, value))[0]


def chunks_of(images):
    if images % 4:
        return [(start, 1) for start in range(images)]
    quarter = images // 4
    return [(0, quarter), (quarter, quarter), (2 * quarter, 2 * quarter)]


def calls_of(chunks):
    return [(0, 1), (2,)] if len(chunks) == 3 else [(n,) for n in range(len(chunks))]


def all_weights(local):
    groups = lax.axis_size("group")
    rows = local.shape[0] // groups
    part = lax.dynamic_slice_in_dim(local, lax.axis_index("group") * rows, rows, 0)
    return lax.all_gather(part, ("swap", "group"), axis=0, tiled=True)


def total_over_swap(parts, me, share):
    mine = lax.dynamic_index_in_dim(share, me, 0, keepdims=False)
    got = [
        lax.ppermute(
            lax.dynamic_index_in_dim(share, lax.bitwise_xor(me, k), 0, keepdims=False),
            "swap",
            across(parts, k),
        )
        for k in range(parts - 1, 0, -1)
    ]
    for piece in got:
        mine = mine + piece
    whole = jnp.zeros(share.shape, share.dtype)
    whole = lax.dynamic_update_index_in_dim(whole, mine, me, 0)
    for k in range(parts - 1, 0, -1):
        piece = lax.ppermute(mine, "swap", across(parts, k))
        whole = lax.dynamic_update_index_in_dim(whole, piece, lax.bitwise_xor(me, k), 0)
    return whole


def shards_kernels(
    parts,
    images_in,
    kernel,
    conv_bias,
    norm_gain,
    norm_shift,
    fp8_weight,
    block_scale,
    adapter_a,
    adapter_b,
    cotangent,
):
    me = lax.axis_index("swap")
    side = lax.axis_index("image")
    place = jnp.stack([me, side]).astype(jnp.int32)
    weight = all_weights(decode(fp8_weight, block_scale))
    channels = images_in.shape[1]
    coefs = jnp.broadcast_to(
        kernel.T.astype(jnp.float32)[:, :, None], (KS * KS, channels, LANES)
    )
    bias = jnp.broadcast_to(conv_bias[:, None], (channels, LANES))
    gain, shift = norm_gain[:, None], norm_shift[:, None]
    table = shift_table()
    chunks = chunks_of(images_in.shape[0])
    held = []
    for start, count in chunks:
        pieces = conv_images(start, count, place, images_in, coefs, bias, table, parts)
        place = after(place, pieces[0])
        held.append((pieces[:-1], lax.ppermute(pieces[-1], "swap", across(parts, 1))))
    own = []
    for n, (start, count) in enumerate(chunks):
        near, far = held[n]
        if n + 1 < len(chunks):
            far = after(far, held[n + 1][0][0])
        both = [jnp.stack([near[k], far[k]]) for k in range(parts // 2)]
        arrived = [both[0]] + [
            lax.ppermute(both[k], "swap", across(parts, 2 * k)) for k in range(1, parts // 2)
        ]
        own.append((start, count, arrived))
    grad_a, grad_b = [], []
    for group in calls_of(chunks):
        mine, theirs = [], []
        for n in group:
            start, _, arrived = own[n]
            mine.append(norm_images(start, place, arrived, gain, shift))
            theirs.append(lax.ppermute(mine[-1], "image", [(0, 1), (1, 0)]))
            place = after(place, mine[-1])
        start = chunks[group[0]][0]
        one_a, one_b = main_chunk(
            start, place, mine, theirs, weight, adapter_a, adapter_b, cotangent
        )
        place = after(place, one_b)
        grad_a.append(one_a)
        grad_b.append(one_b)
    rank = adapter_a.shape[1]
    sum_a, sum_b = sum(grad_a[1:], grad_a[0]), sum(grad_b[1:], grad_b[0])
    half = sum_a.shape[1] // 2
    halves = sum_a.reshape(rank, 2, half).swapaxes(0, 1)
    kept = lax.dynamic_index_in_dim(halves, side, 0, keepdims=False)
    given = lax.dynamic_index_in_dim(halves, 1 - side, 0, keepdims=False)
    kept = kept + lax.ppermute(given, "image", [(0, 1), (1, 0)])
    joined = jnp.concatenate([kept, sum_b], axis=1)
    share = joined.reshape(rank, parts, -1).swapaxes(0, 1)
    whole = total_over_swap(parts, me, share).swapaxes(0, 1).reshape(rank, -1)
    kept, sum_b = whole[:, :half], whole[:, half:]
    given = lax.ppermute(kept, "image", [(0, 1), (1, 0)])
    low = jnp.where(side == 0, kept, given)
    high = jnp.where(side == 0, given, kept)
    return jnp.concatenate([low, high], axis=1).T, sum_b


def shards_plain(
    images_in,
    kernel,
    conv_bias,
    norm_gain,
    norm_shift,
    fp8_weight,
    block_scale,
    adapter_a,
    adapter_b,
    cotangent,
):
    batch, channels, pixels = images_in.shape
    maps = images_in.reshape(batch, channels, pixels // W, W)
    conv = lax.conv_general_dilated(
        maps,
        kernel.reshape(channels, 1, KS, KS),
        (1, 1),
        ((HALF, HALF), (HALF, HALF)),
        dimension_numbers=("NCHW", "OIHW", "NCHW"),
        feature_group_count=channels,
        preferred_element_type=jnp.float32,
    ).reshape(batch, channels, pixels)
    conv = (conv + conv_bias[None, :, None]).astype(jnp.bfloat16)
    values = lax.all_to_all(conv, "swap", split_axis=2, concat_axis=1, tiled=True).astype(
        jnp.float32
    )
    average = jnp.mean(values, axis=1, keepdims=True)
    centred = values - average
    variance = jnp.mean(centred * centred, axis=1, keepdims=True)
    scaled = (
        centred * lax.rsqrt(variance + norm_eps) * norm_gain[None, :, None]
        + norm_shift[None, :, None]
    )
    normed = jnp.swapaxes(scaled, 1, 2).astype(jnp.bfloat16)
    own_rows = normed.reshape(-1, normed.shape[2])
    tokens = lax.all_gather(own_rows, "image", axis=0, tiled=True)
    local_weight = decode(fp8_weight, block_scale)
    weight = lax.all_gather(local_weight, "swap", axis=0, tiled=True)
    frozen = jnp.dot(tokens, weight, preferred_element_type=jnp.float32)
    low_rank = jnp.dot(tokens, adapter_a, preferred_element_type=jnp.float32).astype(jnp.bfloat16)
    pre_act = frozen + adapter_scale * jnp.dot(
        low_rank, adapter_b, preferred_element_type=jnp.float32
    )
    upstream = cotangent.reshape(-1, cotangent.shape[2])
    cumulative = 0.5 * (1.0 + jax.scipy.special.erf(pre_act * 0.7071067811865476))
    slope = cumulative + pre_act * (jnp.exp(-0.5 * pre_act * pre_act) * DENSITY)
    grad_pre = (upstream.astype(jnp.float32) * slope).astype(jnp.bfloat16)
    grad_b = adapter_scale * jnp.dot(low_rank.T, grad_pre, preferred_element_type=jnp.float32)
    back = lax.psum(jnp.dot(grad_pre, adapter_b.T, preferred_element_type=jnp.float32), "image")
    grad_a = adapter_scale * lax.dot_general(
        tokens.astype(jnp.float32),
        back,
        (((0,), (0,)), ((), ())),
        precision=lax.Precision.HIGHEST,
        preferred_element_type=jnp.float32,
    )
    return lax.psum((grad_a, grad_b), "swap")


def solution(mesh):
    placed = (
        P(("group", "image"), "swap", None),
        P("swap", None),
        P("swap"),
        P(),
        P(),
        P("swap", "image"),
        P("swap", "image"),
        P(),
        P(None, "image"),
        P("group", "swap", "image"),
    )
    parts = mesh.shape["swap"]

    def body(*shards):
        _, channels, pixels = shards[0].shape
        span = pixels // parts
        fits = (
            2 <= parts <= 8
            and parts & (parts - 1) == 0
            and mesh.shape["image"] == 2
            and channels % 16 == 0
            and span % LANES == 0
            and LANES % W == 0
            and shards[5].shape[1] % LANES == 0
        )
        return functools.partial(shards_kernels, parts)(*shards) if fits else shards_plain(*shards)

    return jax.shard_map(
        body,
        mesh=mesh,
        in_specs=placed,
        out_specs=(P("group", None), P("group", "image")),
        check_vma=False,
    )
```

```python
import functools

import jax
import jax.numpy as jnp
from jax import lax
from jax.experimental import pallas as pl
from jax.experimental.pallas import tpu as pltpu
from jax.sharding import PartitionSpec as P

KS = 7
W = 64
LANES = 128
HALF = KS // 2

adapter_scale = 2.0
norm_eps = 1e-06

TAIL_STEP = 0.275
TAIL = (0.11780931, 0.04211112, 0.33393318, -0.33099448, 0.45199936, -0.11485849)
DENSITY = 0.3989422804014327
VMEM_LIMIT = 56 * 1024 * 1024


def power_table(scales):
    factor = jnp.zeros(scales.shape, jnp.float32)
    for exponent in range(-12, 4):
        factor = factor + jnp.where(
            scales == exponent, jnp.float32(2.0**exponent), jnp.float32(0.0)
        )
    return factor


def decode(weight, scales):
    row_count = weight.shape[0]
    groups = scales.shape[1]
    blocks = (
        weight.reshape(row_count, groups, -1).astype(jnp.float32) * power_table(scales)[:, :, None]
    )
    return blocks.reshape(row_count, -1).astype(jnp.bfloat16)


def params(**more):
    return pltpu.CompilerParams(vmem_limit_bytes=VMEM_LIMIT, **more)


def shift_table():
    shape = (2 * LANES, 2 * KS, LANES)
    source, case, lane = (lax.broadcasted_iota(jnp.int32, shape, axis) for axis in range(3))
    shift = case // 2 - HALF
    column = lane % W + shift
    hit = (source == lane + shift + W * (case % 2)) & (column >= 0) & (column < W)
    return hit.astype(jnp.bfloat16).reshape(shape[0], -1)


def conv_body(where, image, coefs, bias, table, *rest, parts, group):
    outs, (pairs, lines, sums) = rest[: parts // 2 + 1], rest[parts // 2 + 1 :]
    channels, pixels = image.shape[1:]
    tiles = pixels // LANES
    span = pixels // parts
    zero = jnp.zeros((channels, LANES), jnp.bfloat16)

    def tile(t):
        return image[0, :, t * LANES : (t + 1) * LANES] if 0 <= t < tiles else zero

    for t in range(-2, tiles + 1):
        pairs[t + 2, :, :LANES] = tile(t)
        pairs[t + 2, :, LANES:] = tile(t + 1)

    def prepare(start, stop):
        flat = pairs[start:stop].reshape((stop - start) * channels, 2 * LANES)
        moved = jnp.dot(flat, table[...], preferred_element_type=jnp.float32)
        lines[start:stop] = moved.reshape(stop - start, channels, 2 * KS * LANES)

    def add(start, rows):
        total = [bias[rows, :]] * group
        for b in range(KS):
            for odd, steps in ((0, (-2, 0, 2)), (1, (-3, -1, 1, 3))):
                at = slice((2 * b + odd) * LANES, (2 * b + odd + 1) * LANES)
                near = [lines[start + j, rows, at] for j in range(group + 3)]
                for row_step in steps:
                    coef = coefs[(row_step + HALF) * KS + b, rows, :]
                    ahead = 2 + (row_step - odd) // 2
                    for j in range(group):
                        total[j] = total[j] + near[j + ahead] * coef
        for j in range(group):
            sums[rows, (start + j) * LANES : (start + j + 1) * LANES] = total[j]

    done = 0
    for start in range(0, tiles, group):
        for ahead in (0, group):
            stop = min(tiles + 3, start + ahead + group + 3)
            if stop > done:
                prepare(done, stop)
                done = stop
        for row in range(0, channels, 8):
            add(start, slice(row, row + 8))
    for k in range(parts):
        origin = pl.multiple_of(lax.bitwise_xor(where[0], k) * span, LANES)
        block = sums[:, pl.ds(origin, span)].astype(jnp.bfloat16)
        if k % 2:
            outs[-1][k // 2, 0] = block
        else:
            outs[k // 2][0] = block


def conv_images(start, count, place, images, coefs, bias, table, parts):
    _, channels, pixels = images.shape
    rows = 16
    tiles = pixels // LANES
    span = pixels // parts
    return pl.pallas_call(
        functools.partial(conv_body, parts=parts, group=16 if tiles % 16 == 0 else 1),
        grid_spec=pltpu.PrefetchScalarGridSpec(
            num_scalar_prefetch=1,
            grid=(count, channels // rows),
            in_specs=[
                pl.BlockSpec((1, rows, pixels), lambda i, c, place: (start + i, c, 0)),
                pl.BlockSpec((KS * KS, rows, LANES), lambda i, c, place: (0, c, 0)),
                pl.BlockSpec((rows, LANES), lambda i, c, place: (c, 0)),
                pl.BlockSpec((2 * LANES, 2 * KS * LANES), lambda i, c, place: (0, 0)),
            ],
            out_specs=[pl.BlockSpec((1, rows, span), lambda i, c, place: (i, c, 0))] * (parts // 2)
            + [pl.BlockSpec((parts // 2, 1, rows, span), lambda i, c, place: (0, i, c, 0))],
            scratch_shapes=[
                pltpu.VMEM((tiles + 3, rows, 2 * LANES), jnp.bfloat16),
                pltpu.VMEM((tiles + 3, rows, 2 * KS * LANES), jnp.float32),
                pltpu.VMEM((rows, pixels), jnp.float32),
            ],
        ),
        out_shape=[jax.ShapeDtypeStruct((count, channels, span), jnp.bfloat16)] * (parts // 2)
        + [jax.ShapeDtypeStruct((parts // 2, count, channels, span), jnp.bfloat16)],
        compiler_params=params(),
        name=f"conv_{start}",
    )(place, images, coefs, bias, table)


def norm_body(where, *refs, parts):
    pieces, (gain, shift, out, values) = refs[: parts // 2], refs[parts // 2 :]
    rows = pieces[0].shape[2]
    for k in range(parts):
        origin = pl.multiple_of(lax.bitwise_xor(where[0], k) * rows, 16)
        values[pl.ds(origin, rows), :] = pieces[k // 2][k % 2, 0].astype(jnp.float32)
    channels = values.shape[0]
    average = jnp.sum(values[...], axis=0, keepdims=True) * (1.0 / channels)
    centred = values[...] - average
    variance = jnp.sum(centred * centred, axis=0, keepdims=True) * (1.0 / channels)
    scaled = centred * lax.rsqrt(variance + norm_eps) * gain[...] + shift[...]
    out[...] = scaled.astype(jnp.bfloat16).T


def norm_images(start, place, pieces, gain, shift):
    parts = 2 * len(pieces)
    _, count, rows, span = pieces[0].shape
    channels = rows * parts
    return pl.pallas_call(
        functools.partial(norm_body, parts=parts),
        grid_spec=pltpu.PrefetchScalarGridSpec(
            num_scalar_prefetch=1,
            grid=(count,),
            in_specs=[pl.BlockSpec((2, 1, rows, span), lambda i, place: (0, i, 0, 0))] * (parts // 2)
            + [pl.BlockSpec((channels, 1), lambda i, place: (0, 0))] * 2,
            out_specs=pl.BlockSpec((span, channels), lambda i, place: (i, 0)),
            scratch_shapes=[pltpu.VMEM((channels, span), jnp.float32)],
        ),
        out_shape=jax.ShapeDtypeStruct((count * span, channels), jnp.bfloat16),
        compiler_params=params(),
        name=f"norm_{start}",
    )(place, *pieces, gain, shift)


def gelu_slope(x):
    size = jnp.abs(x)
    t = 1.0 / (1.0 + TAIL_STEP * size)
    tail = TAIL[-1]
    for coefficient in TAIL[-2::-1]:
        tail = tail * t + coefficient
    fall = jnp.exp(-0.5 * (x * x)) * (DENSITY * size - tail * t)
    return jnp.where(x >= 0, 1.0 + fall, -fall)


def main_body(where, *refs, step, last_odd, pieces):
    f = pl.program_id(0)
    steps = pl.num_programs(0) - 1
    owns, others, refs = refs[:pieces], refs[pieces : 2 * pieces], refs[2 * pieces :]
    weight, down, up, up_old, cot_own, cot_other, grad_a, grad_b = refs[:8]
    low, low_t, back, pre_even, pre_odd = refs[8:]
    span = cot_own.shape[1]
    rows = cot_own.shape[0] * span
    sides, blocks = [], []
    for side, (group, cot) in enumerate(((owns, cot_own), (others, cot_other))):
        base = 0
        for tokens in group:
            sides.append((tokens, side * rows + base))
            blocks += [
                (tokens, start, cot, base + start, side * rows + base + start)
                for start in range(0, tokens.shape[0], step)
            ]
            base += tokens.shape[0]

    def project(new, block):
        tokens, start, _, _, place = block
        new[place : place + step, :] = jnp.dot(
            tokens[start : start + step, :], weight[...], preferred_element_type=jnp.float32
        ) + jnp.dot(low[place : place + step, :], up[...], preferred_element_type=jnp.float32)

    def finish(old, block):
        _, _, cot, at, place = block
        within = at % span
        upstream = cot[at // span, within : within + step, :].astype(jnp.float32)
        slope = gelu_slope(old[place : place + step, :])
        grad_pre = (upstream * slope).astype(jnp.bfloat16)
        back[:, place : place + step] += lax.dot_general(
            up_old[...], grad_pre, (((1,), (1,)), ((), ())), preferred_element_type=jnp.float32
        )
        return jnp.dot(low_t[:, place : place + step], grad_pre, preferred_element_type=jnp.float32)

    @pl.when(f == 0)
    def first():
        back[...] = jnp.zeros_like(back)
        for tokens, start, _, _, place in blocks:
            product = jnp.dot(
                tokens[start : start + step, :], down[...], preferred_element_type=jnp.float32
            )
            rounded = product.astype(jnp.bfloat16).astype(jnp.float32) * adapter_scale
            low[place : place + step, :] = rounded.astype(jnp.bfloat16)
            low_t[:, place : place + step] = rounded.T.astype(jnp.bfloat16)
        for block in blocks:
            project(pre_even, block)

    def both(new, old):
        total = None
        for block in blocks:
            project(new, block)
            product = finish(old, block)
            total = product if total is None else total + product
        grad_b[...] = total

    inner = (f > 0) & (f < steps)
    pl.when(inner & (f % 2 == 1))(lambda: both(pre_odd, pre_even))
    pl.when(inner & (f % 2 == 0))(lambda: both(pre_even, pre_odd))

    @pl.when(f == steps)
    def last():
        total = None
        for block in blocks:
            product = finish(pre_odd if last_odd else pre_even, block)
            total = product if total is None else total + product
        grad_b[...] = total
        rank = back.shape[0]
        total = None
        for tokens, base in sides:
            wide = back[:, base : base + tokens.shape[0]] * adapter_scale
            high = wide.astype(jnp.bfloat16)
            rest = (wide - high.astype(jnp.float32)).astype(jnp.bfloat16)
            pair = jnp.concatenate([high, rest], axis=0)
            product = jnp.dot(pair, tokens[...], preferred_element_type=jnp.float32)
            total = product if total is None else total + product
        grad_a[...] = total[:rank] + total[rank:]


def main_chunk(index, place, own, other, weight, down, up, cotangent):
    rows, channels = sum(piece.shape[0] for piece in own), own[0].shape[1]
    hidden = weight.shape[1]
    rank = down.shape[1]
    images, span, _ = cotangent.shape
    count = rows // span
    half = images // 2 // count
    at = index // count
    width = 512 if hidden % 512 == 0 else LANES
    step = 256 if span % 256 == 0 else span
    steps = hidden // width

    def now(f):
        return jnp.minimum(f, steps - 1)

    def before(f):
        return jnp.maximum(f - 1, 0)

    return pl.pallas_call(
        functools.partial(main_body, step=step, last_odd=steps % 2 == 0, pieces=len(own)),
        grid_spec=pltpu.PrefetchScalarGridSpec(
            num_scalar_prefetch=1,
            grid=(steps + 1,),
            in_specs=[
                *[pl.BlockSpec(piece.shape, lambda f, place: (0, 0)) for piece in own + other],
                pl.BlockSpec((channels, width), lambda f, place: (0, now(f))),
                pl.BlockSpec((channels, rank), lambda f, place: (0, 0)),
                pl.BlockSpec((rank, width), lambda f, place: (0, now(f))),
                pl.BlockSpec((rank, width), lambda f, place: (0, before(f))),
                pl.BlockSpec((count, span, width), lambda f, place: (place[1] * half + at, 0, before(f))),
                pl.BlockSpec(
                    (count, span, width), lambda f, place: ((1 - place[1]) * half + at, 0, before(f))
                ),
            ],
            out_specs=[
                pl.BlockSpec((rank, channels), lambda f, place: (0, 0)),
                pl.BlockSpec((rank, width), lambda f, place: (0, before(f))),
            ],
            scratch_shapes=[
                pltpu.VMEM((2 * rows, rank), jnp.bfloat16),
                pltpu.VMEM((rank, 2 * rows), jnp.bfloat16),
                pltpu.VMEM((rank, 2 * rows), jnp.float32),
                pltpu.VMEM((2 * rows, width), jnp.float32),
                pltpu.VMEM((2 * rows, width), jnp.float32),
            ],
        ),
        out_shape=[
            jax.ShapeDtypeStruct((rank, channels), jnp.float32),
            jax.ShapeDtypeStruct((rank, hidden), jnp.float32),
        ],
        compiler_params=params(),
        name=f"main_{index}",
    )(place, *own, *other, weight, down, up, up, cotangent, cotangent)


def across(parts, k):
    return [(s, s ^ k) for s in range(parts)]


def after(place, value):
    return lax.optimization_barrier((place, value))[0]


def chunks_of(images):
    if images % 4:
        return [(start, 1) for start in range(images)]
    quarter = images // 4
    return [(0, quarter), (quarter, quarter), (2 * quarter, 2 * quarter)]


def calls_of(chunks):
    return [(0, 1), (2,)] if len(chunks) == 3 else [(n,) for n in range(len(chunks))]


def all_weights(local):
    groups = lax.axis_size("group")
    rows = local.shape[0] // groups
    part = lax.dynamic_slice_in_dim(local, lax.axis_index("group") * rows, rows, 0)
    return lax.all_gather(part, ("swap", "group"), axis=0, tiled=True)


def total_over_swap(parts, me, share):
    mine = lax.dynamic_index_in_dim(share, me, 0, keepdims=False)
    got = [
        lax.ppermute(
            lax.dynamic_index_in_dim(share, lax.bitwise_xor(me, k), 0, keepdims=False),
            "swap",
            across(parts, k),
        )
        for k in range(parts - 1, 0, -1)
    ]
    for piece in got:
        mine = mine + piece
    whole = jnp.zeros(share.shape, share.dtype)
    whole = lax.dynamic_update_index_in_dim(whole, mine, me, 0)
    for k in range(parts - 1, 0, -1):
        piece = lax.ppermute(mine, "swap", across(parts, k))
        whole = lax.dynamic_update_index_in_dim(whole, piece, lax.bitwise_xor(me, k), 0)
    return whole


def shards_kernels(
    parts,
    images_in,
    kernel,
    conv_bias,
    norm_gain,
    norm_shift,
    fp8_weight,
    block_scale,
    adapter_a,
    adapter_b,
    cotangent,
):
    me = lax.axis_index("swap")
    side = lax.axis_index("image")
    place = jnp.stack([me, side]).astype(jnp.int32)
    weight = all_weights(decode(fp8_weight, block_scale))
    channels = images_in.shape[1]
    coefs = jnp.broadcast_to(
        kernel.T.astype(jnp.float32)[:, :, None], (KS * KS, channels, LANES)
    )
    bias = jnp.broadcast_to(conv_bias[:, None], (channels, LANES))
    gain, shift = norm_gain[:, None], norm_shift[:, None]
    table = shift_table()
    chunks = chunks_of(images_in.shape[0])
    held = []
    for start, count in chunks:
        pieces = conv_images(start, count, place, images_in, coefs, bias, table, parts)
        place = after(place, pieces[0])
        held.append((pieces[:-1], lax.ppermute(pieces[-1], "swap", across(parts, 1))))
    own = []
    for n, (start, count) in enumerate(chunks):
        near, far = held[n]
        if n + 1 < len(chunks):
            far = after(far, held[n + 1][0][0])
        both = [jnp.stack([near[k], far[k]]) for k in range(parts // 2)]
        arrived = [both[0]] + [
            lax.ppermute(both[k], "swap", across(parts, 2 * k)) for k in range(1, parts // 2)
        ]
        own.append((start, count, arrived))
    grad_a, grad_b = [], []
    for group in calls_of(chunks):
        tokens = []
        for n in group:
            start, _, arrived = own[n]
            mine = norm_images(start, place, arrived, gain, shift)
            tokens.append((start, mine, lax.ppermute(mine, "image", [(0, 1), (1, 0)])))
            place = after(place, mine)
        for start, mine, theirs in tokens:
            one_a, one_b = main_chunk(
                start, place, [mine], [theirs], weight, adapter_a, adapter_b, cotangent
            )
            place = after(place, one_b)
            grad_a.append(one_a)
            grad_b.append(one_b)
    rank = adapter_a.shape[1]
    sum_a, sum_b = sum(grad_a[1:], grad_a[0]), sum(grad_b[1:], grad_b[0])
    half = sum_a.shape[1] // 2
    halves = sum_a.reshape(rank, 2, half).swapaxes(0, 1)
    kept = lax.dynamic_index_in_dim(halves, side, 0, keepdims=False)
    given = lax.dynamic_index_in_dim(halves, 1 - side, 0, keepdims=False)
    kept = kept + lax.ppermute(given, "image", [(0, 1), (1, 0)])
    joined = jnp.concatenate([kept, sum_b], axis=1)
    share = joined.reshape(rank, parts, -1).swapaxes(0, 1)
    whole = total_over_swap(parts, me, share).swapaxes(0, 1).reshape(rank, -1)
    kept, sum_b = whole[:, :half], whole[:, half:]
    given = lax.ppermute(kept, "image", [(0, 1), (1, 0)])
    low = jnp.where(side == 0, kept, given)
    high = jnp.where(side == 0, given, kept)
    return jnp.concatenate([low, high], axis=1).T, sum_b


def shards_plain(
    images_in,
    kernel,
    conv_bias,
    norm_gain,
    norm_shift,
    fp8_weight,
    block_scale,
    adapter_a,
    adapter_b,
    cotangent,
):
    batch, channels, pixels = images_in.shape
    maps = images_in.reshape(batch, channels, pixels // W, W)
    conv = lax.conv_general_dilated(
        maps,
        kernel.reshape(channels, 1, KS, KS),
        (1, 1),
        ((HALF, HALF), (HALF, HALF)),
        dimension_numbers=("NCHW", "OIHW", "NCHW"),
        feature_group_count=channels,
        preferred_element_type=jnp.float32,
    ).reshape(batch, channels, pixels)
    conv = (conv + conv_bias[None, :, None]).astype(jnp.bfloat16)
    values = lax.all_to_all(conv, "swap", split_axis=2, concat_axis=1, tiled=True).astype(
        jnp.float32
    )
    average = jnp.mean(values, axis=1, keepdims=True)
    centred = values - average
    variance = jnp.mean(centred * centred, axis=1, keepdims=True)
    scaled = (
        centred * lax.rsqrt(variance + norm_eps) * norm_gain[None, :, None]
        + norm_shift[None, :, None]
    )
    normed = jnp.swapaxes(scaled, 1, 2).astype(jnp.bfloat16)
    own_rows = normed.reshape(-1, normed.shape[2])
    tokens = lax.all_gather(own_rows, "image", axis=0, tiled=True)
    local_weight = decode(fp8_weight, block_scale)
    weight = lax.all_gather(local_weight, "swap", axis=0, tiled=True)
    frozen = jnp.dot(tokens, weight, preferred_element_type=jnp.float32)
    low_rank = jnp.dot(tokens, adapter_a, preferred_element_type=jnp.float32).astype(jnp.bfloat16)
    pre_act = frozen + adapter_scale * jnp.dot(
        low_rank, adapter_b, preferred_element_type=jnp.float32
    )
    upstream = cotangent.reshape(-1, cotangent.shape[2])
    cumulative = 0.5 * (1.0 + jax.scipy.special.erf(pre_act * 0.7071067811865476))
    slope = cumulative + pre_act * (jnp.exp(-0.5 * pre_act * pre_act) * DENSITY)
    grad_pre = (upstream.astype(jnp.float32) * slope).astype(jnp.bfloat16)
    grad_b = adapter_scale * jnp.dot(low_rank.T, grad_pre, preferred_element_type=jnp.float32)
    back = lax.psum(jnp.dot(grad_pre, adapter_b.T, preferred_element_type=jnp.float32), "image")
    grad_a = adapter_scale * lax.dot_general(
        tokens.astype(jnp.float32),
        back,
        (((0,), (0,)), ((), ())),
        precision=lax.Precision.HIGHEST,
        preferred_element_type=jnp.float32,
    )
    return lax.psum((grad_a, grad_b), "swap")


def solution(mesh):
    placed = (
        P(("group", "image"), "swap", None),
        P("swap", None),
        P("swap"),
        P(),
        P(),
        P("swap", "image"),
        P("swap", "image"),
        P(),
        P(None, "image"),
        P("group", "swap", "image"),
    )
    parts = mesh.shape["swap"]

    def body(*shards):
        _, channels, pixels = shards[0].shape
        span = pixels // parts
        fits = (
            2 <= parts <= 8
            and parts & (parts - 1) == 0
            and mesh.shape["image"] == 2
            and channels % 16 == 0
            and span % LANES == 0
            and LANES % W == 0
            and shards[5].shape[1] % LANES == 0
        )
        return functools.partial(shards_kernels, parts)(*shards) if fits else shards_plain(*shards)

    return jax.shard_map(
        body,
        mesh=mesh,
        in_specs=placed,
        out_specs=(P("group", None), P("group", "image")),
        check_vma=False,
    )
```
